256 devices in a mesh: gx: 32 (over y, x, core), gy: 8 (over z).
Axes of the slice: x: 4, y: 4, z: 8, core: 2. Of those that a mesh axis runs over, the one named last changes fastest.
Arguments:
- probes: float32 [64, 64, 64, 128], P(None, 'gx', 'gy'), may hold values from -6 to 6
- conduct: float32 [64, 64, 128], P('gx', 'gy'), may hold values from 0.25 to 2
- storage: float32 [64, 64, 128], P('gx', 'gy'), may hold values from 0.5 to 2
Outputs:
- basis: float32 [64, 64, 64, 128], P(None, 'gx', 'gy')
- factor: float32 [64, 64], replicated
The draws below stay inside these ranges and needn't reach their ends.
All inputs are finite; a program needn't handle non-finite values.
Results may differ from the reference program's by a relative error of at most 0.00005.
Values sent between devices are 32-bit elements; how exact they have to be, the bound alone decides.
No kernel may reach another device: no remote copies, remote signals or barrier semaphores. Data moves between devices by JAX's collectives and lax.ppermute only.
A program may use at most 64 MiB of HBM per device.

```python
import math
import jax
import jax.numpy as jnp
from jax import lax

P_SIZE = 64
NZ = 128
STEPS = 8
NX = 64
NY = 64


def steps_of(own_key, shape, pieces, smallest, high):
    def one(position, parts):
        draws = jax.random.uniform(jax.random.fold_in(jax.random.fold_in(own_key, 6), position), (parts,), jnp.float32, smallest / len(pieces), high / len(pieces))
        return jnp.repeat(jnp.exp(draws), shape[position] // parts).reshape((-1,) + (1,) * (len(shape) - position - 1))

    gain = one(*pieces[0])
    for cut in pieces[1:]:
        gain = gain * one(*cut)
    return gain


def scatter_about(stream_key, dims, width, reach, split=(), held_as=jnp.bfloat16):
    drawn = jax.random.normal(stream_key, dims, jnp.float32) * width
    if len(split) > 0:
        drawn = steps_of(stream_key, dims, split, -0.22, 0.18) * drawn
    return jnp.clip(drawn, min=-reach, max=reach).astype(held_as)


def setup_inputs(seed: int = 0) -> dict:
    key_list = jax.random.split(jax.random.key(seed), 4)
    probes = scatter_about(key_list[0], (P_SIZE, NX, NY, NZ), 1.0, 6.0, ((1, 32), (2, 8)), jnp.float32)
    conduct = jnp.clip(jnp.exp(math.log(2.0) - 2.0794415 * jax.random.uniform(key_list[1], (NX, NY, NZ), jnp.float32) ** steps_of(key_list[1], (NX, NY, NZ), ((0, 32), (1, 8)), -0.2, 0.2)), 0.25, 2.0)
    storage = jnp.clip(jnp.exp(math.log(2.0) - 1.3862944 * jax.random.uniform(key_list[2], (NX, NY, NZ), jnp.float32) ** steps_of(key_list[2], (NX, NY, NZ), ((0, 32), (1, 8)), -0.2, 0.2)), 0.5, 2.0)
    return {"probes": probes, "conduct": conduct, "storage": storage}


time_step = 0.07
prior_weight = 0.5

def laplace_full(field):
    padded = jnp.pad(field, ((0, 0), (1, 1), (1, 1), (1, 1)))
    beside = padded[:, 2:, 1:-1, 1:-1] + padded[:, :-2, 1:-1, 1:-1]
    beside = beside + padded[:, 1:-1, 2:, 1:-1] + padded[:, 1:-1, :-2, 1:-1]
    beside = beside + padded[:, 1:-1, 1:-1, 2:] + padded[:, 1:-1, 1:-1, :-2]
    return 6.0 * field - beside

def reference(probes, conduct, storage):
    source = time_step * storage[None] * probes
    forward = source
    for sweep in range(STEPS):
        forward = forward - time_step * laplace_full(conduct[None] * forward) + source
    costate = forward
    summed = forward
    for sweep in range(STEPS):
        costate = costate - time_step * conduct[None] * laplace_full(costate)
        summed = summed + costate
    response = time_step * storage[None] * summed + prior_weight * probes
    flat = response.reshape(P_SIZE, -1)
    gram = jnp.dot(flat, flat.T, precision=lax.Precision.HIGHEST)
    lower = jnp.linalg.cholesky(gram)
    solved = jax.scipy.linalg.solve_triangular(lower, flat, lower=True)
    scale = math.sqrt(NX * NY * NZ)
    return ((solved * scale).reshape(probes.shape), lower.T / scale)
```

```python
import math

import jax
import jax.numpy as jnp
from jax import lax
from jax.experimental import pallas as pl
from jax.experimental.pallas import tpu as pltpu
from jax.sharding import Mesh, PartitionSpec as P

STEPS = 8
time_step = 0.07
prior_weight = 0.5

STRIP = ("tx", "tc", "tz")
ROWS = 16
EXT = 3 * ROWS
TILES = 8
CHUNK = 24


def shifted(value, lane):
    up = jnp.where(lane == 0, 0.0, pltpu.roll(value, 1, 1))
    down = jnp.where(lane == 127, 0.0, pltpu.roll(value, 127, 1))
    return up + down


def flow_kernel(own, before, after, own_c, before_c, after_c, out, coef, src, state, ping, pong):
    core = lax.axis_index("tc")
    lane = lax.broadcasted_iota(jnp.int32, (8, 128), 1)
    sub = lax.broadcasted_iota(jnp.int32, (8, 128), 0)

    def put(buf, x, vals):
        for j in range(8):
            buf[x, j + 1] = vals[j]
        buf[x, 0] = jnp.where(sub == 0, 0.0, pltpu.roll(vals[7], 1, 0))
        buf[x, 9] = jnp.where(sub == 7, 0.0, pltpu.roll(vals[0], 7, 0))

    def neighbours(buf, x, j):
        c = buf[x, j + 1]
        s = (buf[x - 1, j + 1] + buf[x + 1, j + 1]) + (buf[x, j] + buf[x, j + 2])
        return c, s + shifted(c, lane)

    for strip, (block, other) in enumerate(((before, before_c), (own, own_c), (after, after_c))):

        def load(i, _, strip=strip, block=block, other=other):
            row = strip * ROWS + 2 * i
            for j in range(8):
                mine = block[pl.ds(i * (8 * CHUNK) + 16 + j, 8, stride=CHUNK)]
                coef[row + core, j] = time_step * mine
                theirs = other[pl.ds(i * 64 + j, 8, stride=8)]
                coef[row + 1 - core, j] = time_step * theirs
            for a in range(2):
                vals = []
                for j in range(8):
                    s = block[pl.ds(i * (8 * CHUNK) + 8 * a + j, 8, stride=CHUNK)]
                    src[row + a, j] = s
                    state[row + a, j] = s
                    vals.append(coef[row + a, j] * s)
                put(ping, row + a, vals)
            return 0

        lax.fori_loop(0, 8, load, 0)

    bufs = (ping, pong)
    for k in range(1, STEPS + 1):
        now, later = bufs[(k - 1) % 2], bufs[k % 2]

        def forward(x, _, k=k, now=now, later=later):
            vals = []
            for j in range(8):
                c, s = neighbours(now, x, j)
                f = (state[x, j] + src[x, j]) + (s - 6.0 * c)
                a = coef[x, j]
                if k < STEPS:
                    state[x, j] = f
                    vals.append(a * f)
                else:
                    f = jnp.where(a > 0.0, f, 0.0)
                    state[x, j] = f
                    vals.append(f)
            put(later, x, vals)
            return 0

        lax.fori_loop(k, EXT - k, forward, 0)

    for k in range(STEPS + 1, 2 * STEPS + 1):
        now, later = bufs[(k - 1) % 2], bufs[k % 2]

        def adjoint(x, _, k=k, now=now, later=later, keep=False):
            vals = []
            for j in range(8):
                c, s = neighbours(now, x, j)
                w = c + coef[x, j] * (s - 6.0 * c)
                if keep:
                    total = state[x, j] + w
                    if k < 2 * STEPS:
                        state[x, j] = total
                    else:
                        i, a = (x - ROWS) // 2, (x - ROWS) % 2
                        out[pl.ds(i * 128 + a * 8 + j, 8, stride=16)] = total
                vals.append(w)
            if k < 2 * STEPS:
                put(later, x, vals)
            return 0

        if k < 2 * STEPS:
            lax.fori_loop(k, ROWS, adjoint, 0)
            lax.fori_loop(2 * ROWS, EXT - k, adjoint, 0)
        lax.fori_loop(ROWS, 2 * ROWS, lambda x, c, f=adjoint: f(x, c, keep=True), 0)


def gram_kernel(back, probes, storage, flat, packed):
    for r in range(16):
        rows = pl.ds(r, 64, stride=16)
        y = (time_step * storage[r:r + 1, :]) * back[rows] + prior_weight * probes[rows]
        flat[:, r * 128:(r + 1) * 128] = y
    y = flat[...]
    gram = lax.dot_general(y, y, (((1,), (1,)), ((), ())), precision=lax.Precision.HIGHEST, preferred_element_type=jnp.float32)
    dense = jnp.concatenate([gram[:32], gram[32:]], axis=1)
    for i in range(packed.shape[0]):
        packed[i] = dense


def solve_kernel(parts, flat, basis, factor, scale):
    dense = parts[0]
    for i in range(1, parts.shape[0]):
        dense = dense + parts[i]
    gram = jnp.concatenate([dense[:, :64], dense[:, 64:]], axis=0)
    row = lax.broadcasted_iota(jnp.int32, (64, 64), 0)
    col = lax.broadcasted_iota(jnp.int32, (64, 64), 1)
    eye = jnp.where(row == col, 1.0, 0.0)
    work = jnp.concatenate([gram, eye], axis=1)
    rows = lax.broadcasted_iota(jnp.int32, (64, 128), 0)
    diag = jnp.ones((64, 128), jnp.float32)
    for k in range(64):
        pivot_row = work[k:k + 1, :]
        column = jnp.broadcast_to(work[:, k:k + 1], (64, 128))
        pivot = column[k:k + 1, :]
        diag = jnp.where(rows == k, pivot, diag)
        work = work - jnp.where(rows > k, column * (1.0 / pivot), 0.0) * pivot_row
    work = work * lax.rsqrt(diag)
    upper = jnp.where(row <= col, work[:, :64], 0.0)
    factor[...] = upper / scale
    inverse = work[:, 64:] * scale
    solved = lax.dot_general(inverse, flat[...], (((1,), (0,)), ((), ())), precision=lax.Precision.HIGHEST, preferred_element_type=jnp.float32)
    for r in range(16):
        basis[pl.ds(r, 64, stride=16)] = solved[:, r * 128:(r + 1) * 128]


def vmem(n):
    return [pl.BlockSpec(memory_space=pltpu.VMEM)] * n


def params():
    return pltpu.CompilerParams(vmem_limit_bytes=40 * 1024 * 1024)


def shards(probes, conduct, storage):
    f32 = jnp.float32
    source = (time_step * storage[None] * probes).reshape(64, 16, 128)
    halves = jnp.broadcast_to(conduct[None, :, None], (4, 2, 8, 8, 128)).reshape(64, 8, 128)
    sent = jnp.concatenate([source, halves], axis=1)
    own = lax.all_to_all(sent, STRIP, 0, 0, tiled=True)
    up = [(i, i + 1) for i in range(3)]
    down = [(j, i) for i, j in up]
    before = lax.ppermute(own, "ty", up)
    after = lax.ppermute(own, "ty", down)
    swap = [(0, 1), (1, 0)]
    others = [lax.ppermute(a[:, 16:], "tc", swap).reshape(512, 128) for a in (own, before, after)]
    blocks = [a.reshape(64 * CHUNK, 128) for a in (own, before, after)]
    summed = pl.pallas_call(
        flow_kernel,
        out_shape=jax.ShapeDtypeStruct((1024, 128), f32),
        in_specs=vmem(6),
        out_specs=vmem(1)[0],
        scratch_shapes=[
            pltpu.VMEM((EXT, 8, 8, 128), f32),
            pltpu.VMEM((EXT, 8, 8, 128), f32),
            pltpu.VMEM((EXT, 8, 8, 128), f32),
            pltpu.VMEM((EXT, 10, 8, 128), f32),
            pltpu.VMEM((EXT, 10, 8, 128), f32),
        ],
        compiler_params=params(),
        name="flow",
    )(*blocks, *others)
    back = lax.all_to_all(summed.reshape(64, 16, 128), STRIP, 0, 0, tiled=True)
    flat, packed = pl.pallas_call(
        gram_kernel,
        out_shape=(jax.ShapeDtypeStruct((64, 2048), f32), jax.ShapeDtypeStruct((16, 32, 128), f32)),
        in_specs=vmem(3),
        out_specs=tuple(vmem(2)),
        compiler_params=params(),
        name="gram",
    )(back.reshape(1024, 128), probes.reshape(1024, 128), storage.reshape(16, 128))
    parts = lax.all_to_all(packed, ("ty", "tx"), 0, 0, tiled=True)
    parts = jnp.broadcast_to(parts.sum(0)[None], (16, 32, 128))
    parts = lax.all_to_all(parts, ("tc", "tz"), 0, 0, tiled=True)
    scale = math.sqrt(64 * 64 * 128)

    def solve(*refs):
        solve_kernel(*refs, scale)

    basis, factor = pl.pallas_call(
        solve,
        out_shape=(jax.ShapeDtypeStruct((1024, 128), f32), jax.ShapeDtypeStruct((64, 64), f32)),
        in_specs=vmem(2),
        out_specs=tuple(vmem(2)),
        compiler_params=params(),
        name="solve",
    )(parts, flat)
    return basis.reshape(probes.shape), factor


def solution(mesh):
    fine = Mesh(mesh.devices.reshape(4, 4, 2, 8), ("ty", "tx", "tc", "tz"))
    gx = ("ty", "tx", "tc")
    placed = (P(None, gx, "tz", None), P(gx, "tz", None), P(gx, "tz", None))
    return jax.shard_map(
        shards,
        mesh=fine,
        in_specs=placed,
        out_specs=(P(None, gx, "tz", None), P()),
        check_vma=False,
    )
```

```python
import math

import jax
import jax.numpy as jnp
from jax import lax
from jax.experimental import pallas as pl
from jax.experimental.pallas import tpu as pltpu
from jax.sharding import Mesh, PartitionSpec as P

STEPS = 8
time_step = 0.07
prior_weight = 0.5

OWN = 8
EXT = 3 * OWN
CHUNK = 40

f32 = jnp.float32


def pack_kernel(got, first, second, half):
    for y in range(OWN):
        for j in range(8):
            row = (j // 2) * CHUNK + (j % 2) * 8 + y
            first[y, j] = got[pl.ds(row, 8, stride=4 * CHUNK)]
            second[y, j] = got[pl.ds(row + 16, 8, stride=4 * CHUNK)]
        for i in range(4):
            half[y, i] = got[pl.ds(i * CHUNK + 32 + y, 8, stride=4 * CHUNK)]


def coef_kernel(m0, m1, m2, t0, t1, t2, coef, stay):
    core = lax.axis_index("tc")
    for strip, (mine, theirs) in enumerate(((m0, t0), (m1, t1), (m2, t2))):
        for y in range(OWN):
            for i in range(4):
                for ref, j in ((mine, 2 * i + core), (theirs, 2 * i + 1 - core)):
                    a = time_step * ref[y, i]
                    coef[strip * OWN + y, j] = a
                    stay[strip * OWN + y, j] = 1.0 - 6.0 * a


def masks():
    lane = lax.broadcasted_iota(jnp.int32, (8, 128), 1)
    sub = lax.broadcasted_iota(jnp.int32, (8, 128), 0)
    return lane == 0, lane == 127, sub == 0, sub == 7


def put(buf, y, vals, m):
    for j in range(8):
        buf[y, j + 1] = vals[j]
    buf[y, 0] = jnp.where(m[2], 0.0, pltpu.roll(vals[7], 1, 0))
    buf[y, 9] = jnp.where(m[3], 0.0, pltpu.roll(vals[0], 7, 0))


def row_sums(buf, y, m):
    row = [buf[y, j] for j in range(10)]
    out = []
    for j in range(8):
        c = row[j + 1]
        up = jnp.where(m[0], 0.0, pltpu.roll(c, 1, 1))
        down = jnp.where(m[1], 0.0, pltpu.roll(c, 127, 1))
        s = (buf[y - 1, j + 1] + buf[y + 1, j + 1]) + (row[j] + row[j + 2]) + (up + down)
        out.append((c, s))
    return out


def forward_kernel(before, own, after, coef, stay, out, scaled, ping, pong):
    m = masks()
    for strip, ref in enumerate((before, own, after)):
        for y in range(OWN):
            vals = []
            for j in range(8):
                v = coef[strip * OWN + y, j] * ref[y, j]
                scaled[strip * OWN + y, j] = v
                vals.append(v)
            put(ping, strip * OWN + y, vals, m)
    bufs = (ping, pong)
    for k in range(1, STEPS):
        now, later = bufs[(k - 1) % 2], bufs[k % 2]
        for y in range(k, EXT - k):
            vals = []
            for j, (c, s) in enumerate(row_sums(now, y, m)):
                vals.append((scaled[y, j] + stay[y, j] * c) + coef[y, j] * s)
            put(later, y, vals, m)
    now = bufs[(STEPS - 1) % 2]
    for y in range(OWN, 2 * OWN):
        for j, (c, s) in enumerate(row_sums(now, y, m)):
            out[y - OWN, j] = (own[y - OWN, j] + c / coef[y, j]) + (s - 6.0 * c)


def adjoint(before, own, after, coef, stay, total, ping, pong, finish):
    m = masks()
    for strip, ref in enumerate((before, own, after)):
        for y in range(OWN):
            put(ping, strip * OWN + y, [ref[y, j] for j in range(8)], m)
    bufs = (ping, pong)
    for k in range(1, STEPS + 1):
        now, later = bufs[(k - 1) % 2], bufs[k % 2]
        for y in range(k, EXT - k):
            vals = []
            for j, (c, s) in enumerate(row_sums(now, y, m)):
                w = stay[y, j] * c + coef[y, j] * s
                vals.append(w)
                if OWN <= y < 2 * OWN:
                    i = y - OWN
                    t = (own[i, j] if k == 1 else total[i, j]) + w
                    if k < STEPS:
                        total[i, j] = t
                    else:
                        finish(i, j, t)
            if k < STEPS:
                put(later, y, vals, m)


def adjoint_first_kernel(before, own, after, coef, stay, out, total, ping, pong):
    def finish(y, j, t):
        out[y, j] = t

    adjoint(before, own, after, coef, stay, total, ping, pong, finish)


def adjoint_second_kernel(before, own, after, coef, stay, first, out, total, ping, pong):
    def row(y, j, probe):
        return pl.ds((j // 2) * 32 + probe * 16 + (j % 2) * 8 + y, 8, stride=128)

    def finish(y, j, t):
        out[row(y, j, 0)] = first[y, j]
        out[row(y, j, 1)] = t

    adjoint(before, own, after, coef, stay, total, ping, pong, finish)


def gram_kernel(back, probes, storage, flat, packed):
    for r in range(16):
        rows = pl.ds(r, 64, stride=16)
        y = (time_step * storage[r:r + 1, :]) * back[rows] + prior_weight * probes[rows]
        flat[:, r * 128:(r + 1) * 128] = y
    y = flat[...]
    gram = lax.dot_general(y, y, (((1,), (1,)), ((), ())), precision=lax.Precision.HIGHEST, preferred_element_type=f32)
    packed[...] = jnp.concatenate([gram[:32], gram[32:]], axis=1)


def solve_kernel(parts, flat, basis, factor, scale):
    dense = parts[0]
    for i in range(1, parts.shape[0]):
        dense = dense + parts[i]
    gram = jnp.concatenate([dense[:, :64], dense[:, 64:]], axis=0)
    row = lax.broadcasted_iota(jnp.int32, (64, 64), 0)
    col = lax.broadcasted_iota(jnp.int32, (64, 64), 1)
    eye = jnp.where(row == col, 1.0, 0.0)
    work = jnp.concatenate([gram, eye], axis=1)
    rows = lax.broadcasted_iota(jnp.int32, (64, 128), 0)
    diag = jnp.ones((64, 128), f32)
    for k in range(64):
        pivot_row = work[k:k + 1, :]
        column = jnp.broadcast_to(work[:, k:k + 1], (64, 128))
        pivot = column[k:k + 1, :]
        diag = jnp.where(rows == k, pivot, diag)
        work = work - jnp.where(rows > k, column * (1.0 / pivot), 0.0) * pivot_row
    work = work * lax.rsqrt(diag)
    upper = jnp.where(row <= col, work[:, :64], 0.0)
    factor[...] = upper / scale
    inverse = work[:, 64:] * scale
    solved = lax.dot_general(inverse, flat[...], (((1,), (0,)), ((), ())), precision=lax.Precision.HIGHEST, preferred_element_type=f32)
    for r in range(16):
        basis[pl.ds(r, 64, stride=16)] = solved[:, r * 128:(r + 1) * 128]


def shape(*dims):
    return jax.ShapeDtypeStruct(dims, f32)


def call(kernel, outs, *args, scratch=(), flops=0, name):
    spec = pl.BlockSpec(memory_space=pltpu.VMEM)
    many = isinstance(outs, tuple)
    moved = 4 * sum(a.size for a in args)
    return pl.pallas_call(
        kernel,
        out_shape=outs,
        in_specs=[spec] * len(args),
        out_specs=tuple([spec] * len(outs)) if many else spec,
        scratch_shapes=[pltpu.VMEM(s, f32) for s in scratch],
        compiler_params=pltpu.CompilerParams(vmem_limit_bytes=32 * 1024 * 1024),
        cost_estimate=pl.CostEstimate(flops=flops, bytes_accessed=moved, transcendentals=0),
        name=name,
    )(*args)


def shards(probes, conduct, storage):
    source = (time_step * storage[None] * probes).reshape(32, 32, 128)
    halves = jnp.broadcast_to(conduct[None], (16, 2, 8, 128)).reshape(32, 8, 128)
    got = lax.all_to_all(jnp.concatenate([source, halves], axis=1), ("ty", "tx", "tc"), 0, 0, tiled=True)
    field = shape(OWN, 8, 8, 128)
    first, second, half = call(
        pack_kernel, (field, field, shape(OWN, 4, 8, 128)), got.reshape(32 * CHUNK, 128), name="pack"
    )
    up = [(i, i + 1) for i in range(7)]
    down = [(j, i) for i, j in up]

    def sides(a):
        return lax.ppermute(a, "tz", up), a, lax.ppermute(a, "tz", down)

    def swap(a):
        return lax.ppermute(a, "tc", [(0, 1), (1, 0)])

    halfs = sides(half)
    fields = [sides(first), sides(second)]
    wide = shape(EXT, 8, 8, 128)
    coefs = call(coef_kernel, (wide, wide), *halfs, *[swap(h) for h in halfs], name="coef")
    pads = ((EXT, 10, 8, 128),) * 2
    work = 14 * 120 * 8 * 1024
    forward = [
        call(forward_kernel, field, *f, *coefs, scratch=(wide.shape,) + pads, flops=work, name="forward") for f in fields
    ]
    forward = [sides(f) for f in forward]
    scratch = (field.shape,) + pads
    total = call(adjoint_first_kernel, field, *forward[0], *coefs, scratch=scratch, flops=work, name="adjoint1")
    summed = call(adjoint_second_kernel, shape(1024, 128), *forward[1], *coefs, total, scratch=scratch, flops=work, name="adjoint2")
    back = lax.all_to_all(summed.reshape(32, 32, 128), ("ty", "tx", "tc"), 0, 0, tiled=True)
    flat, gram = call(
        gram_kernel,
        (shape(64, 2048), shape(32, 128)),
        back.reshape(1024, 128),
        probes.reshape(1024, 128),
        storage.reshape(16, 128),
        name="gram",
    )
    gram = gram + swap(gram)
    parts = lax.all_to_all(jnp.broadcast_to(gram[None], (16, 32, 128)), ("ty", "tx"), 0, 0, tiled=True)
    parts = lax.all_to_all(jnp.broadcast_to(parts.sum(0)[None], (8, 32, 128)), "tz", 0, 0, tiled=True)
    scale = math.sqrt(64 * 64 * 128)

    def solve(*refs):
        solve_kernel(*refs, scale)

    basis, factor = call(solve, (shape(1024, 128), shape(64, 64)), parts, flat, name="solve")
    return basis.reshape(probes.shape), factor


def solution(mesh):
    fine = Mesh(mesh.devices.reshape(4, 4, 2, 8), ("ty", "tx", "tc", "tz"))
    gx = ("ty", "tx", "tc")
    placed = (P(None, gx, "tz", None), P(gx, "tz", None), P(gx, "tz", None))
    return jax.shard_map(
        shards,
        mesh=fine,
        in_specs=placed,
        out_specs=(P(None, gx, "tz", None), P()),
        check_vma=False,
    )
```

```python
import math

import jax
import jax.numpy as jnp
from jax import lax
from jax.experimental import pallas as pl
from jax.experimental.pallas import tpu as pltpu
from jax.sharding import Mesh, PartitionSpec as P

STEPS = 8
time_step = 0.07
prior_weight = 0.5

OWN = 8
EXT = 3 * OWN
CHUNK = 40

f32 = jnp.float32


def send_kernel(probes_hbm, conduct_hbm, storage_hbm, out, probes, conduct, storage, sems):
    pairs = ((storage_hbm, storage), (probes_hbm, probes), (conduct_hbm, conduct))
    copies = [pltpu.make_async_copy(a, b, sems.at[i]) for i, (a, b) in enumerate(pairs)]
    for copy in copies:
        copy.start()
    for copy in copies:
        copy.wait()
    weight = time_step * storage[...]
    for g in range(32):
        out[g, 0:16] = weight * probes[2 * g]
        out[g, 16:32] = weight * probes[2 * g + 1]
        out[g, 32:40] = conduct[8 * (g % 2):8 * (g % 2) + 8]


def pack_kernel(got, half, first, second):
    for y in range(OWN):
        for i in range(4):
            half[y, i] = got[pl.ds(i * CHUNK + 32 + y, 8, stride=4 * CHUNK)]
        for j in range(8):
            row = (j // 2) * CHUNK + (j % 2) * 8 + y
            first[y, j] = got[pl.ds(row, 8, stride=4 * CHUNK)]
            second[y, j] = got[pl.ds(row + 16, 8, stride=4 * CHUNK)]


def strips(own, pair, other):
    odd = lax.rem(lax.axis_index("tz"), 2)
    return ((own, OWN), (pair, 2 * OWN * (1 - odd)), (other, 2 * OWN * odd))


def coef_kernel(m0, m1, m2, t0, t1, t2, coef, stay):
    core = lax.axis_index("tc")
    for (mine, theirs), row in strips((m0, t0), (m1, t1), (m2, t2)):
        for y in range(OWN):
            for i in range(4):
                for v, j in ((mine[y, i], 2 * i + core), (theirs[y, i], 2 * i + 1 - core)):
                    a = time_step * v
                    coef[row + y, j] = a
                    stay[row + y, j] = 1.0 - 6.0 * a


def masks():
    lane = lax.broadcasted_iota(jnp.int32, (8, 128), 1)
    sub = lax.broadcasted_iota(jnp.int32, (8, 128), 0)
    return lane == 0, lane == 127, sub == 0, sub == 7


def put(buf, y, vals, m):
    for j in range(8):
        buf[y, j + 1] = vals[j]
    buf[y, 0] = jnp.where(m[2], 0.0, pltpu.roll(vals[7], 1, 0))
    buf[y, 9] = jnp.where(m[3], 0.0, pltpu.roll(vals[0], 7, 0))


def row_sums(buf, y, m):
    row = [buf[y, j] for j in range(10)]
    out = []
    for j in range(8):
        c = row[j + 1]
        up = jnp.where(m[0], 0.0, pltpu.roll(c, 1, 1))
        down = jnp.where(m[1], 0.0, pltpu.roll(c, 127, 1))
        s = (buf[y - 1, j + 1] + buf[y + 1, j + 1]) + (row[j] + row[j + 2]) + (up + down)
        out.append((c, s))
    return out


def forward_kernel(own, pair, other, coef, stay, out, scaled, ping, pong):
    m = masks()
    for ref, row in strips(own, pair, other):
        for y in range(OWN):
            vals = []
            for j in range(8):
                v = coef[row + y, j] * ref[y, j]
                scaled[row + y, j] = v
                vals.append(v)
            put(ping, row + y, vals, m)
    bufs = (ping, pong)
    for k in range(1, STEPS):
        now, later = bufs[(k - 1) % 2], bufs[k % 2]
        for y in range(k, EXT - k):
            vals = []
            for j, (c, s) in enumerate(row_sums(now, y, m)):
                vals.append((scaled[y, j] + stay[y, j] * c) + coef[y, j] * s)
            put(later, y, vals, m)
    now = bufs[(STEPS - 1) % 2]
    for y in range(OWN, 2 * OWN):
        for j, (c, s) in enumerate(row_sums(now, y, m)):
            out[y - OWN, j] = (own[y - OWN, j] + c / coef[y, j]) + (s - 6.0 * c)


def adjoint(own, pair, other, coef, stay, total, ping, pong, finish):
    m = masks()
    for ref, row in strips(own, pair, other):
        for y in range(OWN):
            put(ping, row + y, [ref[y, j] for j in range(8)], m)
    bufs = (ping, pong)
    for k in range(1, STEPS + 1):
        now, later = bufs[(k - 1) % 2], bufs[k % 2]
        for y in range(k, EXT - k):
            vals = []
            for j, (c, s) in enumerate(row_sums(now, y, m)):
                w = stay[y, j] * c + coef[y, j] * s
                vals.append(w)
                if OWN <= y < 2 * OWN:
                    i = y - OWN
                    t = (own[i, j] if k == 1 else total[i, j]) + w
                    if k < STEPS:
                        total[i, j] = t
                    else:
                        finish(i, j, t)
            if k < STEPS:
                put(later, y, vals, m)


def adjoint_first_kernel(own, pair, other, coef, stay, out, total, ping, pong):
    def finish(y, j, t):
        out[y, j] = t

    adjoint(own, pair, other, coef, stay, total, ping, pong, finish)


def adjoint_second_kernel(own, pair, other, coef, stay, first, out, total, ping, pong):
    def row(y, j, probe):
        return pl.ds((j // 2) * 32 + probe * 16 + (j % 2) * 8 + y, 8, stride=128)

    def finish(y, j, t):
        out[row(y, j, 0)] = first[y, j]
        out[row(y, j, 1)] = t

    adjoint(own, pair, other, coef, stay, total, ping, pong, finish)


def gram_kernel(back, probes, storage, flat, packed):
    for r in range(16):
        rows = pl.ds(r, 64, stride=16)
        y = (time_step * storage[r:r + 1, :]) * back[rows] + prior_weight * probes[rows]
        flat[:, r * 128:(r + 1) * 128] = y
    y = flat[...]
    gram = lax.dot_general(y, y, (((1,), (1,)), ((), ())), precision=lax.Precision.HIGHEST, preferred_element_type=f32)
    packed[...] = jnp.concatenate([gram[:32], gram[32:]], axis=1)


def solve_kernel(parts, flat, basis, factor, scale):
    dense = parts[0]
    for i in range(1, parts.shape[0]):
        dense = dense + parts[i]
    gram = jnp.concatenate([dense[:, :64], dense[:, 64:]], axis=0)
    row = lax.broadcasted_iota(jnp.int32, (64, 64), 0)
    col = lax.broadcasted_iota(jnp.int32, (64, 64), 1)
    eye = jnp.where(row == col, 1.0, 0.0)
    work = jnp.concatenate([gram, eye], axis=1)
    rows = lax.broadcasted_iota(jnp.int32, (64, 128), 0)
    diag = jnp.ones((64, 128), f32)
    for first in range(0, 64, 8):
        columns, factors, pivots = [], [], []
        for k in range(first, first + 8):
            column = jnp.broadcast_to(work[:, k:k + 1], (64, 128))
            pivot_row = work[k:k + 1, :]
            for c, f, p in zip(columns, factors, pivots):
                column = column - f * c[k:k + 1, :]
                pivot_row = pivot_row - f[k:k + 1, :] * p
            pivot = column[k:k + 1, :]
            diag = jnp.where(rows == k, pivot, diag)
            columns.append(column)
            factors.append(jnp.where(rows > k, column * (1.0 / pivot), 0.0))
            pivots.append(pivot_row)
        for f, p in zip(factors, pivots):
            work = work - f * p
    work = work * lax.rsqrt(diag)
    upper = jnp.where(row <= col, work[:, :64], 0.0)
    factor[...] = upper / scale
    inverse = work[:, 64:] * scale
    solved = lax.dot_general(inverse, flat[...], (((1,), (0,)), ((), ())), precision=lax.Precision.HIGHEST, preferred_element_type=f32)
    for r in range(16):
        basis[pl.ds(r, 64, stride=16)] = solved[:, r * 128:(r + 1) * 128]


def shape(*dims):
    return jax.ShapeDtypeStruct(dims, f32)


def call(kernel, outs, *args, scratch=(), sems=0, places=None, limit=32 * 1024 * 1024, flops=0, name):
    spec = pl.BlockSpec(memory_space=pltpu.VMEM)
    many = isinstance(outs, tuple)
    return pl.pallas_call(
        kernel,
        out_shape=outs,
        in_specs=[pl.BlockSpec(memory_space=p) for p in places or [pltpu.VMEM] * len(args)],
        out_specs=tuple([spec] * len(outs)) if many else spec,
        scratch_shapes=[pltpu.VMEM(s, f32) for s in scratch] + [pltpu.SemaphoreType.DMA((sems,))] * (sems > 0),
        compiler_params=pltpu.CompilerParams(vmem_limit_bytes=limit),
        cost_estimate=pl.CostEstimate(flops=flops, bytes_accessed=4 * sum(a.size for a in args), transcendentals=0),
        name=name,
    )(*args)


def shards(probes, conduct, storage):
    probes, conduct, storage = probes.reshape(64, 16, 128), conduct.reshape(16, 128), storage.reshape(16, 128)
    sent = call(
        send_kernel,
        shape(32, CHUNK, 128),
        probes,
        conduct,
        storage,
        scratch=(probes.shape, conduct.shape, storage.shape),
        sems=3,
        places=[pltpu.HBM] * 3,
        limit=None,
        name="send",
    )
    got = lax.all_to_all(sent, ("ty", "tx", "tc"), 0, 0, tiled=True)
    field = shape(OWN, 8, 8, 128)
    got = got.reshape(32 * CHUNK, 128)
    half, first, second = call(pack_kernel, (shape(OWN, 4, 8, 128), field, field), got, name="pack")
    exchanges = [[(i, i + 1) for i in range(k, 7, 2)] for k in range(2)]
    exchanges = [e + [(j, i) for i, j in e] for e in exchanges]

    def sides(a):
        return [a] + [lax.ppermute(a, "tz", e) for e in exchanges]

    def swap(a):
        return lax.ppermute(a, "tc", [(0, 1), (1, 0)])

    halfs = sides(half)
    fields = [sides(first), sides(second)]
    wide = shape(EXT, 8, 8, 128)
    coefs = call(coef_kernel, (wide, wide), *halfs, *[swap(a) for a in halfs], name="coef")
    pads = ((EXT, 10, 8, 128),) * 2
    work = 14 * 120 * 8 * 1024
    forward = [
        call(forward_kernel, field, *f, *coefs, scratch=(wide.shape,) + pads, flops=work, name="forward") for f in fields
    ]
    forward = [sides(f) for f in forward]
    scratch = (field.shape,) + pads
    total = call(adjoint_first_kernel, field, *forward[0], *coefs, scratch=scratch, flops=work, name="adjoint1")
    summed = call(adjoint_second_kernel, shape(1024, 128), *forward[1], *coefs, total, scratch=scratch, flops=work, name="adjoint2")
    back = lax.all_to_all(summed.reshape(32, 32, 128), ("ty", "tx", "tc"), 0, 0, tiled=True)
    flat, gram = call(
        gram_kernel,
        (shape(64, 2048), shape(32, 128)),
        back.reshape(1024, 128),
        probes.reshape(1024, 128),
        storage,
        name="gram",
    )
    gram = gram + swap(gram)
    parts = lax.all_to_all(jnp.broadcast_to(gram[None], (16, 32, 128)), ("ty", "tx"), 0, 0, tiled=True)
    parts = lax.all_to_all(jnp.broadcast_to(parts.sum(0)[None], (8, 32, 128)), "tz", 0, 0, tiled=True)
    scale = math.sqrt(64 * 64 * 128)

    def solve(*refs):
        solve_kernel(*refs, scale)

    basis, factor = call(solve, (shape(1024, 128), shape(64, 64)), parts, flat, name="solve")
    return basis.reshape(64, 2, 8, 128), factor


def solution(mesh):
    fine = Mesh(mesh.devices.reshape(4, 4, 2, 8), ("ty", "tx", "tc", "tz"))
    gx = ("ty", "tx", "tc")
    placed = (P(None, gx, "tz", None), P(gx, "tz", None), P(gx, "tz", None))
    return jax.shard_map(
        shards,
        mesh=fine,
        in_specs=placed,
        out_specs=(P(None, gx, "tz", None), P()),
        check_vma=False,
    )
```

```python
import functools
import math

import jax
import jax.numpy as jnp
from jax import lax
from jax.experimental import pallas as pl
from jax.experimental.pallas import tpu as pltpu
from jax.sharding import Mesh, PartitionSpec as P

STEPS = 8
time_step = 0.07
prior_weight = 0.5

OWN = 8
EXT = 3 * OWN
CHUNK = 40

f32 = jnp.float32


def send_kernel(probes_hbm, conduct_hbm, storage_hbm, out, probes, conduct, storage, sems):
    pairs = ((storage_hbm, storage), (probes_hbm, probes), (conduct_hbm, conduct))
    copies = [pltpu.make_async_copy(a, b, sems.at[i]) for i, (a, b) in enumerate(pairs)]
    for copy in copies:
        copy.start()
    for copy in copies:
        copy.wait()
    weight = time_step * storage[...]
    for g in range(32):
        out[g, 0:16] = weight * probes[2 * g]
        out[g, 16:32] = weight * probes[2 * g + 1]
        out[g, 32:40] = conduct[8 * (g % 2):8 * (g % 2) + 8]


def pack_kernel(got, half, first):
    for y in range(OWN):
        for i in range(4):
            half[y, i] = got[pl.ds(i * CHUNK + 32 + y, 8, stride=4 * CHUNK)]
        for j in range(8):
            first[y, j] = got[pl.ds((j // 2) * CHUNK + (j % 2) * 8 + y, 8, stride=4 * CHUNK)]


def pack_second_kernel(got, arrived, out):
    for y in range(OWN):
        for j in range(8):
            out[y, j] = got[pl.ds((j // 2) * CHUNK + 16 + (j % 2) * 8 + y, 8, stride=4 * CHUNK)]


def strips(own, pair, other):
    odd = lax.rem(lax.axis_index("tz"), 2)
    return ((own, OWN), (pair, 2 * OWN * (1 - odd)), (other, 2 * OWN * odd))


def coef_kernel(m0, m1, m2, t0, t1, t2, coef, stay):
    core = lax.axis_index("tc")
    for (mine, theirs), row in strips((m0, t0), (m1, t1), (m2, t2)):
        for y in range(OWN):
            for i in range(4):
                for v, j in ((mine[y, i], 2 * i + core), (theirs[y, i], 2 * i + 1 - core)):
                    a = time_step * v
                    coef[row + y, j] = a
                    stay[row + y, j] = 1.0 - 6.0 * a


def masks():
    sub = lax.broadcasted_iota(jnp.int32, (8, 128), 0)
    return band(), None, sub == 0, sub == 7


def put(buf, y, vals, m):
    for j in range(8):
        buf[y, j + 1] = vals[j]
    buf[y, 0] = jnp.where(m[2], 0.0, pltpu.roll(vals[7], 1, 0))
    buf[y, 9] = jnp.where(m[3], 0.0, pltpu.roll(vals[0], 7, 0))


def band():
    row = lax.broadcasted_iota(jnp.int32, (256, 128), 0) % 128
    col = lax.broadcasted_iota(jnp.int32, (256, 128), 1)
    return jnp.where(jnp.abs(row - col) == 1, 1.0, 0.0).astype(jnp.bfloat16)


def row_sums(buf, y, m):
    row = [buf[y, j] for j in range(10)]
    whole = jnp.concatenate(row[1:9], axis=0)
    high = whole.astype(jnp.bfloat16)
    low = (whole - high.astype(f32)).astype(jnp.bfloat16)
    along = jnp.dot(jnp.concatenate([high, low], axis=1), m[0], preferred_element_type=f32)
    out = []
    for j in range(8):
        s = (buf[y - 1, j + 1] + buf[y + 1, j + 1]) + (row[j] + row[j + 2]) + along[8 * j:8 * j + 8]
        out.append((row[j + 1], s))
    return out


def forward_kernel(own, pair, other, coef, stay, out, scaled, ping, pong):
    m = masks()
    for ref, row in strips(own, pair, other):
        for y in range(OWN):
            vals = []
            for j in range(8):
                v = coef[row + y, j] * ref[y, j]
                scaled[row + y, j] = v
                vals.append(v)
            put(ping, row + y, vals, m)
    bufs = (ping, pong)
    for k in range(1, STEPS):
        now, later = bufs[(k - 1) % 2], bufs[k % 2]
        for y in range(k, EXT - k):
            vals = []
            for j, (c, s) in enumerate(row_sums(now, y, m)):
                vals.append((scaled[y, j] + stay[y, j] * c) + coef[y, j] * s)
            put(later, y, vals, m)
    now = bufs[(STEPS - 1) % 2]
    for y in range(OWN, 2 * OWN):
        for j, (c, s) in enumerate(row_sums(now, y, m)):
            out[y - OWN, j] = (own[y - OWN, j] + c / coef[y, j]) + (s - 6.0 * c)


def adjoint(own, pair, other, coef, stay, total, ping, pong, finish):
    m = masks()
    for ref, row in strips(own, pair, other):
        for y in range(OWN):
            put(ping, row + y, [ref[y, j] for j in range(8)], m)
    bufs = (ping, pong)
    for k in range(1, STEPS + 1):
        now, later = bufs[(k - 1) % 2], bufs[k % 2]
        for y in range(k, EXT - k):
            vals = []
            for j, (c, s) in enumerate(row_sums(now, y, m)):
                w = stay[y, j] * c + coef[y, j] * s
                vals.append(w)
                if OWN <= y < 2 * OWN:
                    i = y - OWN
                    t = (own[i, j] if k == 1 else total[i, j]) + w
                    if k < STEPS:
                        total[i, j] = t
                    else:
                        finish(i, j, t)
            if k < STEPS:
                put(later, y, vals, m)


def back_row(y, j, probe):
    return pl.ds((j // 2) * 32 + probe * 16 + (j % 2) * 8 + y, 8, stride=128)


def adjoint_kernel(probe, own, pair, other, coef, stay, *refs):
    out, total, ping, pong = refs[-4:]

    def finish(y, j, t):
        out[back_row(y, j, probe)] = t

    adjoint(own, pair, other, coef, stay, total, ping, pong, finish)


def gram_kernel(back, probes, storage, flat, packed):
    for r in range(16):
        rows = pl.ds(r, 64, stride=16)
        y = (time_step * storage[r:r + 1, :]) * back[rows] + prior_weight * probes[rows]
        flat[:, r * 128:(r + 1) * 128] = y
    y = flat[...]
    gram = lax.dot_general(y, y, (((1,), (1,)), ((), ())), precision=lax.Precision.HIGHEST, preferred_element_type=f32)
    packed[...] = jnp.concatenate([gram[:32], gram[32:]], axis=1)


def solve_kernel(parts, flat, basis, factor, scale):
    dense = parts[0]
    for i in range(1, parts.shape[0]):
        dense = dense + parts[i]
    gram = jnp.concatenate([dense[:, :64], dense[:, 64:]], axis=0)
    row = lax.broadcasted_iota(jnp.int32, (64, 64), 0)
    col = lax.broadcasted_iota(jnp.int32, (64, 64), 1)
    eye = jnp.where(row == col, 1.0, 0.0)
    work = jnp.concatenate([gram, eye], axis=1)
    rows = lax.broadcasted_iota(jnp.int32, (64, 128), 0)
    diag = jnp.ones((64, 128), f32)
    for first in range(0, 64, 8):
        columns, factors, pivots = [], [], []
        for k in range(first, first + 8):
            column = jnp.broadcast_to(work[:, k:k + 1], (64, 128))
            pivot_row = work[k:k + 1, :]
            for c, f, p in zip(columns, factors, pivots):
                column = column - f * c[k:k + 1, :]
                pivot_row = pivot_row - f[k:k + 1, :] * p
            pivot = column[k:k + 1, :]
            diag = jnp.where(rows == k, pivot, diag)
            columns.append(column)
            factors.append(jnp.where(rows > k, column * (1.0 / pivot), 0.0))
            pivots.append(pivot_row)
        for f, p in zip(factors, pivots):
            work = work - f * p
    work = work * lax.rsqrt(diag)
    upper = jnp.where(row <= col, work[:, :64], 0.0)
    factor[...] = upper / scale
    inverse = work[:, 64:] * scale
    solved = lax.dot_general(inverse, flat[...], (((1,), (0,)), ((), ())), precision=lax.Precision.HIGHEST, preferred_element_type=f32)
    for r in range(16):
        basis[pl.ds(r, 64, stride=16)] = solved[:, r * 128:(r + 1) * 128]


def shape(*dims):
    return jax.ShapeDtypeStruct(dims, f32)


def call(kernel, outs, *args, scratch=(), sems=0, places=None, limit=32 * 1024 * 1024, flops=0, alias={}, name):
    spec = pl.BlockSpec(memory_space=pltpu.VMEM)
    many = isinstance(outs, tuple)
    return pl.pallas_call(
        kernel,
        out_shape=outs,
        in_specs=[pl.BlockSpec(memory_space=p) for p in places or [pltpu.VMEM] * len(args)],
        out_specs=tuple([spec] * len(outs)) if many else spec,
        scratch_shapes=[pltpu.VMEM(s, f32) for s in scratch] + [pltpu.SemaphoreType.DMA((sems,))] * (sems > 0),
        compiler_params=pltpu.CompilerParams(vmem_limit_bytes=limit),
        cost_estimate=pl.CostEstimate(flops=1024, bytes_accessed=1024, transcendentals=0),
        input_output_aliases=alias,
        name=name,
    )(*args)


def shards(probes, conduct, storage):
    probes, conduct, storage = probes.reshape(64, 16, 128), conduct.reshape(16, 128), storage.reshape(16, 128)
    sent = call(
        send_kernel,
        shape(32, CHUNK, 128),
        probes,
        conduct,
        storage,
        scratch=(probes.shape, conduct.shape, storage.shape),
        sems=3,
        places=[pltpu.HBM] * 3,
        limit=None,
        name="send",
    )
    got = lax.all_to_all(sent, ("ty", "tx", "tc"), 0, 0, tiled=True)
    field = shape(OWN, 8, 8, 128)
    got = got.reshape(32 * CHUNK, 128)
    half, first = call(pack_kernel, (shape(OWN, 4, 8, 128), field), got, name="pack")
    exchanges = [[(i, i + 1) for i in range(k, 7, 2)] for k in range(2)]
    exchanges = [e + [(j, i) for i, j in e] for e in exchanges]

    def sides(a):
        return [a] + [lax.ppermute(a, "tz", e) for e in exchanges]

    def swap(a):
        return lax.ppermute(a, "tc", [(0, 1), (1, 0)])

    halfs = sides(half)
    fields = [sides(first)]
    second = call(pack_second_kernel, field, got, fields[0][1], places=[pltpu.VMEM, pl.ANY], name="pack2")
    fields.append(sides(second))
    wide = shape(EXT, 8, 8, 128)
    coefs = call(coef_kernel, (wide, wide), *halfs, *[swap(a) for a in halfs], name="coef")
    pads = ((EXT, 10, 8, 128),) * 2
    work = 14 * 120 * 8 * 1024
    forward = [
        call(forward_kernel, field, *f, *coefs, scratch=(wide.shape,) + pads, flops=work, name="forward") for f in fields
    ]
    forward = [sides(f) for f in forward]
    scratch = (field.shape,) + pads
    summed = call(
        functools.partial(adjoint_kernel, 0), shape(1024, 128), *forward[0], *coefs, scratch=scratch, flops=work, name="adjoint1"
    )
    summed = call(
        functools.partial(adjoint_kernel, 1),
        shape(1024, 128),
        *forward[1],
        *coefs,
        summed,
        scratch=scratch,
        flops=work,
        alias={5: 0},
        name="adjoint2",
    )
    back = lax.all_to_all(summed.reshape(32, 32, 128), ("ty", "tx", "tc"), 0, 0, tiled=True)
    flat, gram = call(
        gram_kernel,
        (shape(64, 2048), shape(32, 128)),
        back.reshape(1024, 128),
        probes.reshape(1024, 128),
        storage,
        name="gram",
    )
    gram = gram + swap(gram)
    parts = lax.all_to_all(jnp.broadcast_to(gram[None], (16, 32, 128)), ("ty", "tx"), 0, 0, tiled=True)
    parts = lax.all_to_all(jnp.broadcast_to(parts.sum(0)[None], (8, 32, 128)), "tz", 0, 0, tiled=True)
    scale = math.sqrt(64 * 64 * 128)

    def solve(*refs):
        solve_kernel(*refs, scale)

    basis, factor = call(solve, (shape(1024, 128), shape(64, 64)), parts, flat, name="solve")
    return basis.reshape(64, 2, 8, 128), factor


def solution(mesh):
    fine = Mesh(mesh.devices.reshape(4, 4, 2, 8), ("ty", "tx", "tc", "tz"))
    gx = ("ty", "tx", "tc")
    placed = (P(None, gx, "tz", None), P(gx, "tz", None), P(gx, "tz", None))
    return jax.shard_map(
        shards,
        mesh=fine,
        in_specs=placed,
        out_specs=(P(None, gx, "tz", None), P()),
        check_vma=False,
    )
```

```python
import functools
import math

import jax
import jax.numpy as jnp
from jax import lax
from jax.experimental import pallas as pl
from jax.experimental.pallas import tpu as pltpu
from jax.sharding import Mesh, PartitionSpec as P

STEPS = 8
time_step = 0.07
prior_weight = 0.5

OWN = 8
EXT = 3 * OWN
CHUNK = 40

f32 = jnp.float32


def send_kernel(probes_hbm, conduct_hbm, storage_hbm, out, probes, conduct, storage, sems):
    pairs = ((storage_hbm, storage), (probes_hbm, probes), (conduct_hbm, conduct))
    copies = [pltpu.make_async_copy(a, b, sems.at[i]) for i, (a, b) in enumerate(pairs)]
    for copy in copies:
        copy.start()
    for copy in copies:
        copy.wait()
    weight = time_step * storage[...]
    for g in range(32):
        out[g, 0:16] = weight * probes[2 * g]
        out[g, 16:32] = weight * probes[2 * g + 1]
        out[g, 32:40] = conduct[8 * (g % 2):8 * (g % 2) + 8]


def pack_kernel(got, half, first):
    for y in range(OWN):
        for i in range(4):
            half[y, i] = got[pl.ds(i * CHUNK + 32 + y, 8, stride=4 * CHUNK)]
        for j in range(8):
            first[y, j] = got[pl.ds((j // 2) * CHUNK + (j % 2) * 8 + y, 8, stride=4 * CHUNK)]


def pack_second_kernel(got, arrived, out):
    for y in range(OWN):
        for j in range(8):
            out[y, j] = got[pl.ds((j // 2) * CHUNK + 16 + (j % 2) * 8 + y, 8, stride=4 * CHUNK)]


def strips(own, pair, other):
    odd = lax.rem(lax.axis_index("tz"), 2)
    return ((own, OWN), (pair, 2 * OWN * (1 - odd)), (other, 2 * OWN * odd))


def coef_kernel(m0, m1, m2, t0, t1, t2, coef, stay):
    core = lax.axis_index("tc")
    for (mine, theirs), row in strips((m0, t0), (m1, t1), (m2, t2)):
        for y in range(OWN):
            for i in range(4):
                for v, j in ((mine[y, i], 2 * i + core), (theirs[y, i], 2 * i + 1 - core)):
                    a = time_step * v
                    coef[row + y, j] = a
                    stay[row + y, j] = 1.0 - 6.0 * a


def masks():
    sub = lax.broadcasted_iota(jnp.int32, (8, 128), 0)
    return band(), None, sub == 0, sub == 7


def put(buf, y, vals, m):
    for j in range(8):
        buf[y, j + 1] = vals[j]
    buf[y, 0] = jnp.where(m[2], 0.0, pltpu.roll(vals[7], 1, 0))
    buf[y, 9] = jnp.where(m[3], 0.0, pltpu.roll(vals[0], 7, 0))


def band():
    row = lax.broadcasted_iota(jnp.int32, (256, 128), 0) % 128
    col = lax.broadcasted_iota(jnp.int32, (256, 128), 1)
    return jnp.where(jnp.abs(row - col) == 1, 1.0, 0.0).astype(jnp.bfloat16)


def row_sums(buf, y, m):
    row = [buf[y, j] for j in range(10)]
    whole = jnp.concatenate(row[1:9], axis=0)
    high = whole.astype(jnp.bfloat16)
    low = (whole - high.astype(f32)).astype(jnp.bfloat16)
    along = jnp.dot(jnp.concatenate([high, low], axis=1), m[0], preferred_element_type=f32)
    out = []
    for j in range(8):
        s = (buf[y - 1, j + 1] + buf[y + 1, j + 1]) + (row[j] + row[j + 2]) + along[8 * j:8 * j + 8]
        out.append((row[j + 1], s))
    return out


def forward_kernel(own, pair, other, coef, stay, out, scaled, ping, pong):
    m = masks()
    for ref, row in strips(own, pair, other):
        for y in range(OWN):
            vals = []
            for j in range(8):
                v = coef[row + y, j] * ref[y, j]
                scaled[row + y, j] = v
                vals.append(v)
            put(ping, row + y, vals, m)
    bufs = (ping, pong)
    for k in range(1, STEPS):
        now, later = bufs[(k - 1) % 2], bufs[k % 2]
        for y in range(k, EXT - k):
            vals = []
            for j, (c, s) in enumerate(row_sums(now, y, m)):
                vals.append((scaled[y, j] + stay[y, j] * c) + coef[y, j] * s)
            put(later, y, vals, m)
    now = bufs[(STEPS - 1) % 2]
    for y in range(OWN, 2 * OWN):
        for j, (c, s) in enumerate(row_sums(now, y, m)):
            out[y - OWN, j] = (own[y - OWN, j] + c / coef[y, j]) + (s - 6.0 * c)


def adjoint(own, pair, other, coef, stay, total, ping, pong, finish):
    m = masks()
    for ref, row in strips(own, pair, other):
        for y in range(OWN):
            put(ping, row + y, [ref[y, j] for j in range(8)], m)
    bufs = (ping, pong)
    for k in range(1, STEPS + 1):
        now, later = bufs[(k - 1) % 2], bufs[k % 2]
        for y in range(k, EXT - k):
            vals = []
            for j, (c, s) in enumerate(row_sums(now, y, m)):
                w = stay[y, j] * c + coef[y, j] * s
                vals.append(w)
                if OWN <= y < 2 * OWN:
                    i = y - OWN
                    t = (own[i, j] if k == 1 else total[i, j]) + w
                    if k < STEPS:
                        total[i, j] = t
                    else:
                        finish(i, j, t)
            if k < STEPS:
                put(later, y, vals, m)


def back_row(y, j, probe):
    return pl.ds((j // 2) * 32 + probe * 16 + (j % 2) * 8 + y, 8, stride=128)


def adjoint_kernel(probe, own, pair, other, coef, stay, *refs):
    out, total, ping, pong = refs[-4:]

    def finish(y, j, t):
        out[back_row(y, j, probe)] = t

    adjoint(own, pair, other, coef, stay, total, ping, pong, finish)


def gram_kernel(back, probes, storage, flat, packed):
    for r in range(16):
        rows = pl.ds(r, 64, stride=16)
        y = (time_step * storage[r:r + 1, :]) * back[rows] + prior_weight * probes[rows]
        flat[:, r * 128:(r + 1) * 128] = y
    y = flat[...]
    gram = lax.dot_general(y, y, (((1,), (1,)), ((), ())), precision=lax.Precision.HIGHEST, preferred_element_type=f32)
    for i, block in enumerate((gram[:32, :32], gram[:32, 32:], gram[32:, 32:])):
        packed[8 * i:8 * i + 8] = jnp.concatenate([block[8 * k:8 * k + 8] for k in range(4)], axis=1)


def thirds(value):
    parts = []
    for _ in range(3):
        parts.append(value.astype(jnp.bfloat16))
        value = value - parts[-1].astype(f32)
    return parts


def solve_kernel(parts, flat, basis, factor, scale):
    dense = parts[0]
    for i in range(1, parts.shape[0]):
        dense = dense + parts[i]
    blocks = [
        jnp.concatenate([dense[8 * i:8 * i + 8, 32 * k:32 * k + 32] for k in range(4)], axis=0) for i in range(3)
    ]
    gram = jnp.concatenate(
        [jnp.concatenate(blocks[:2], axis=1), jnp.concatenate([blocks[1].T, blocks[2]], axis=1)], axis=0
    )
    row = lax.broadcasted_iota(jnp.int32, (64, 64), 0)
    col = lax.broadcasted_iota(jnp.int32, (64, 64), 1)
    eye = jnp.where(row == col, 1.0, 0.0)
    work = jnp.concatenate([gram, eye], axis=1)
    rows = lax.broadcasted_iota(jnp.int32, (64, 128), 0)
    diag = jnp.ones((64, 128), f32)
    for first in range(0, 64, 8):
        columns, factors, pivots = [], [], []
        for k in range(first, first + 8):
            column = jnp.broadcast_to(work[:, k:k + 1], (64, 128))
            pivot_row = work[k:k + 1, :]
            for c, f, p in zip(columns, factors, pivots):
                column = column - f * c[k:k + 1, :]
                pivot_row = pivot_row - f[k:k + 1, :] * p
            pivot = column[k:k + 1, :]
            diag = jnp.where(rows == k, pivot, diag)
            columns.append(column)
            factors.append(jnp.where(rows > k, column * (1.0 / pivot), 0.0))
            pivots.append(pivot_row)
        for f, p in zip(factors, pivots):
            work = work - f * p
    work = work * lax.rsqrt(diag)
    upper = jnp.where(row <= col, work[:, :64], 0.0)
    factor[...] = upper / scale
    inverse = work[:, 64:] * scale
    a, b = thirds(inverse), thirds(flat[...])
    pairs = ((0, 0), (0, 1), (1, 0), (1, 1), (0, 2), (2, 0))
    left = jnp.concatenate([a[i] for i, _ in pairs], axis=1)
    right = jnp.concatenate([b[j] for _, j in pairs], axis=0)
    solved = jnp.dot(left, right, preferred_element_type=f32)
    for r in range(16):
        basis[pl.ds(r, 64, stride=16)] = solved[:, r * 128:(r + 1) * 128]


def shape(*dims):
    return jax.ShapeDtypeStruct(dims, f32)


def call(kernel, outs, *args, scratch=(), sems=0, places=None, limit=32 * 1024 * 1024, flops=0, alias={}, name):
    spec = pl.BlockSpec(memory_space=pltpu.VMEM)
    many = isinstance(outs, tuple)
    return pl.pallas_call(
        kernel,
        out_shape=outs,
        in_specs=[pl.BlockSpec(memory_space=p) for p in places or [pltpu.VMEM] * len(args)],
        out_specs=tuple([spec] * len(outs)) if many else spec,
        scratch_shapes=[pltpu.VMEM(s, f32) for s in scratch] + [pltpu.SemaphoreType.DMA((sems,))] * (sems > 0),
        compiler_params=pltpu.CompilerParams(vmem_limit_bytes=limit),
        cost_estimate=pl.CostEstimate(flops=1024, bytes_accessed=1024, transcendentals=0),
        input_output_aliases=alias,
        name=name,
    )(*args)


def shards(probes, conduct, storage):
    probes, conduct, storage = probes.reshape(64, 16, 128), conduct.reshape(16, 128), storage.reshape(16, 128)
    sent = call(
        send_kernel,
        shape(32, CHUNK, 128),
        probes,
        conduct,
        storage,
        scratch=(probes.shape, conduct.shape, storage.shape),
        sems=3,
        places=[pltpu.HBM] * 3,
        limit=None,
        name="send",
    )
    got = lax.all_to_all(sent, ("ty", "tx", "tc"), 0, 0, tiled=True)
    field = shape(OWN, 8, 8, 128)
    got = got.reshape(32 * CHUNK, 128)
    half, first = call(pack_kernel, (shape(OWN, 4, 8, 128), field), got, name="pack")
    exchanges = [[(i, i + 1) for i in range(k, 7, 2)] for k in range(2)]
    exchanges = [e + [(j, i) for i, j in e] for e in exchanges]

    def sides(a):
        return [a] + [lax.ppermute(a, "tz", e) for e in exchanges]

    def swap(a):
        return lax.ppermute(a, "tc", [(0, 1), (1, 0)])

    halfs = sides(half)
    fields = [sides(first)]
    second = call(pack_second_kernel, field, got, fields[0][1], places=[pltpu.VMEM, pl.ANY], name="pack2")
    fields.append(sides(second))
    wide = shape(EXT, 8, 8, 128)
    coefs = call(coef_kernel, (wide, wide), *halfs, *[swap(a) for a in halfs], name="coef")
    pads = ((EXT, 10, 8, 128),) * 2
    work = 14 * 120 * 8 * 1024
    forward = [
        call(forward_kernel, field, *f, *coefs, scratch=(wide.shape,) + pads, flops=work, name="forward") for f in fields
    ]
    forward = [sides(f) for f in forward]
    scratch = (field.shape,) + pads
    summed = call(
        functools.partial(adjoint_kernel, 0), shape(1024, 128), *forward[0], *coefs, scratch=scratch, flops=work, name="adjoint1"
    )
    summed = call(
        functools.partial(adjoint_kernel, 1),
        shape(1024, 128),
        *forward[1],
        *coefs,
        summed,
        scratch=scratch,
        flops=work,
        alias={5: 0},
        name="adjoint2",
    )
    back = lax.all_to_all(summed.reshape(32, 32, 128), ("ty", "tx", "tc"), 0, 0, tiled=True)
    flat, gram = call(
        gram_kernel,
        (shape(64, 2048), shape(24, 128)),
        back.reshape(1024, 128),
        probes.reshape(1024, 128),
        storage,
        name="gram",
    )
    gram = gram + swap(gram)
    parts = lax.all_to_all(jnp.broadcast_to(gram[None], (16, 24, 128)), ("ty", "tx"), 0, 0, tiled=True)
    parts = lax.all_to_all(jnp.broadcast_to(parts.sum(0)[None], (8, 24, 128)), "tz", 0, 0, tiled=True)
    scale = math.sqrt(64 * 64 * 128)

    def solve(*refs):
        solve_kernel(*refs, scale)

    basis, factor = call(solve, (shape(1024, 128), shape(64, 64)), parts, flat, name="solve")
    return basis.reshape(64, 2, 8, 128), factor


def solution(mesh):
    fine = Mesh(mesh.devices.reshape(4, 4, 2, 8), ("ty", "tx", "tc", "tz"))
    gx = ("ty", "tx", "tc")
    placed = (P(None, gx, "tz", None), P(gx, "tz", None), P(gx, "tz", None))
    return jax.shard_map(
        shards,
        mesh=fine,
        in_specs=placed,
        out_specs=(P(None, gx, "tz", None), P()),
        check_vma=False,
    )
```

```python
import functools
import math

import jax
import jax.numpy as jnp
from jax import lax
from jax.experimental import pallas as pl
from jax.experimental.pallas import tpu as pltpu
from jax.sharding import Mesh, PartitionSpec as P

STEPS = 8
time_step = 0.07
prior_weight = 0.5

OWN = 8
EXT = 3 * OWN
CHUNK = 40

f32 = jnp.float32


def send_kernel(probes_hbm, conduct_hbm, storage_hbm, out, probes, conduct, storage, sems):
    pairs = ((storage_hbm, storage), (probes_hbm, probes), (conduct_hbm, conduct))
    copies = [pltpu.make_async_copy(a, b, sems.at[i]) for i, (a, b) in enumerate(pairs)]
    for copy in copies:
        copy.start()
    for copy in copies:
        copy.wait()
    weight = time_step * storage[...]
    for g in range(32):
        out[g, 0:16] = weight * probes[2 * g]
        out[g, 16:32] = weight * probes[2 * g + 1]
        out[g, 32:40] = conduct[8 * (g % 2):8 * (g % 2) + 8]


def pack_kernel(got, half, first):
    for y in range(OWN):
        for i in range(4):
            half[y, i] = got[pl.ds(i * CHUNK + 32 + y, 8, stride=4 * CHUNK)]
        for j in range(8):
            first[y, j] = got[pl.ds((j // 2) * CHUNK + (j % 2) * 8 + y, 8, stride=4 * CHUNK)]


def pack_second_kernel(got, arrived, out):
    for y in range(OWN):
        for j in range(8):
            out[y, j] = got[pl.ds((j // 2) * CHUNK + 16 + (j % 2) * 8 + y, 8, stride=4 * CHUNK)]


def strips(own, pair, other):
    odd = lax.rem(lax.axis_index("tz"), 2)
    return ((own, OWN), (pair, 2 * OWN * (1 - odd)), (other, 2 * OWN * odd))


def coef_kernel(m0, m1, m2, t0, t1, t2, coef, stay):
    core = lax.axis_index("tc")
    for (mine, theirs), row in strips((m0, t0), (m1, t1), (m2, t2)):
        for y in range(OWN):
            for i in range(4):
                for v, j in ((mine[y, i], 2 * i + core), (theirs[y, i], 2 * i + 1 - core)):
                    a = time_step * v
                    coef[row + y, j] = a
                    stay[row + y, j] = 1.0 - 6.0 * a


def masks():
    sub = lax.broadcasted_iota(jnp.int32, (8, 128), 0)
    return band(), None, sub == 0, sub == 7


def put(buf, y, vals, m):
    for j in range(8):
        buf[y, j + 1] = vals[j]
    buf[y, 0] = jnp.where(m[2], 0.0, pltpu.roll(vals[7], 1, 0))
    buf[y, 9] = jnp.where(m[3], 0.0, pltpu.roll(vals[0], 7, 0))


def band():
    row = lax.broadcasted_iota(jnp.int32, (256, 128), 0) % 128
    col = lax.broadcasted_iota(jnp.int32, (256, 128), 1)
    return jnp.where(jnp.abs(row - col) == 1, 1.0, 0.0).astype(jnp.bfloat16)


def row_sums(buf, y, m):
    row = [buf[y, j] for j in range(10)]
    whole = jnp.concatenate(row[1:9], axis=0)
    high = whole.astype(jnp.bfloat16)
    low = (whole - high.astype(f32)).astype(jnp.bfloat16)
    along = jnp.dot(jnp.concatenate([high, low], axis=1), m[0], preferred_element_type=f32)
    out = []
    for j in range(8):
        s = (buf[y - 1, j + 1] + buf[y + 1, j + 1]) + (row[j] + row[j + 2]) + along[8 * j:8 * j + 8]
        out.append((row[j + 1], s))
    return out


def forward_kernel(own, pair, other, coef, stay, out, scaled, ping, pong):
    m = masks()
    for ref, row in strips(own, pair, other):
        for y in range(OWN):
            vals = []
            for j in range(8):
                v = coef[row + y, j] * ref[y, j]
                scaled[row + y, j] = v
                vals.append(v)
            put(ping, row + y, vals, m)
    bufs = (ping, pong)
    for k in range(1, STEPS):
        now, later = bufs[(k - 1) % 2], bufs[k % 2]
        for y in range(k, EXT - k):
            vals = []
            for j, (c, s) in enumerate(row_sums(now, y, m)):
                vals.append((scaled[y, j] + stay[y, j] * c) + coef[y, j] * s)
            put(later, y, vals, m)
    now = bufs[(STEPS - 1) % 2]
    for y in range(OWN, 2 * OWN):
        for j, (c, s) in enumerate(row_sums(now, y, m)):
            out[y - OWN, j] = (own[y - OWN, j] + c / coef[y, j]) + (s - 6.0 * c)


def adjoint(own, pair, other, coef, stay, total, ping, pong, finish):
    m = masks()
    for ref, row in strips(own, pair, other):
        for y in range(OWN):
            put(ping, row + y, [ref[y, j] for j in range(8)], m)
    bufs = (ping, pong)
    for k in range(1, STEPS + 1):
        now, later = bufs[(k - 1) % 2], bufs[k % 2]
        for y in range(k, EXT - k):
            vals = []
            for j, (c, s) in enumerate(row_sums(now, y, m)):
                w = stay[y, j] * c + coef[y, j] * s
                vals.append(w)
                if OWN <= y < 2 * OWN:
                    i = y - OWN
                    t = (own[i, j] if k == 1 else total[i, j]) + w
                    if k < STEPS:
                        total[i, j] = t
                    else:
                        finish(i, j, t)
            if k < STEPS:
                put(later, y, vals, m)


def back_row(y, j, probe):
    return pl.ds((j // 2) * 32 + probe * 16 + (j % 2) * 8 + y, 8, stride=128)


def adjoint_kernel(probe, own, pair, other, coef, stay, *refs):
    out, total, ping, pong = refs[-4:]

    def finish(y, j, t):
        out[back_row(y, j, probe)] = t

    adjoint(own, pair, other, coef, stay, total, ping, pong, finish)


def gram_kernel(back, probes, storage, flat, packed):
    for r in range(16):
        rows = pl.ds(r, 64, stride=16)
        y = (time_step * storage[r:r + 1, :]) * back[rows] + prior_weight * probes[rows]
        flat[:, r * 128:(r + 1) * 128] = y
    y = flat[...]
    stack = jnp.concatenate(thirds(y), axis=0)
    p = lax.dot_general(stack, stack, (((1,), (1,)), ((), ())), preferred_element_type=f32)
    low = (p[:64, 128:] + p[128:, :64]) + p[64:128, 64:128]
    gram = p[:64, :64] + ((p[:64, 64:128] + p[64:128, :64]) + low)
    for i, block in enumerate((gram[:32, :32], gram[:32, 32:], gram[32:, 32:])):
        packed[8 * i:8 * i + 8] = jnp.concatenate([block[8 * k:8 * k + 8] for k in range(4)], axis=1)


def thirds(value):
    parts = []
    for _ in range(3):
        parts.append(value.astype(jnp.bfloat16))
        value = value - parts[-1].astype(f32)
    return parts


def solve_kernel(parts, flat, basis, factor, scale):
    dense = parts[0]
    for i in range(1, parts.shape[0]):
        dense = dense + parts[i]
    blocks = [
        jnp.concatenate([dense[8 * i:8 * i + 8, 32 * k:32 * k + 32] for k in range(4)], axis=0) for i in range(3)
    ]
    gram = jnp.concatenate(
        [jnp.concatenate(blocks[:2], axis=1), jnp.concatenate([blocks[1].T, blocks[2]], axis=1)], axis=0
    )
    row = lax.broadcasted_iota(jnp.int32, (64, 64), 0)
    col = lax.broadcasted_iota(jnp.int32, (64, 64), 1)
    eye = jnp.where(row == col, 1.0, 0.0)
    work = jnp.concatenate([gram, eye], axis=1)
    rows = lax.broadcasted_iota(jnp.int32, (64, 128), 0)
    diag = jnp.ones((64, 128), f32)
    for first in range(0, 64, 8):
        columns, factors, pivots = [], [], []
        for k in range(first, first + 8):
            column = jnp.broadcast_to(work[:, k:k + 1], (64, 128))
            pivot_row = work[k:k + 1, :]
            for c, f, p in zip(columns, factors, pivots):
                column = column - f * c[k:k + 1, :]
                pivot_row = pivot_row - f[k:k + 1, :] * p
            pivot = column[k:k + 1, :]
            diag = jnp.where(rows == k, pivot, diag)
            columns.append(column)
            factors.append(jnp.where(rows > k, column * (1.0 / pivot), 0.0))
            pivots.append(pivot_row)
        for f, p in zip(factors, pivots):
            work = work - f * p
    work = work * lax.rsqrt(diag)
    upper = jnp.where(row <= col, work[:, :64], 0.0)
    factor[...] = upper / scale
    inverse = work[:, 64:] * scale
    a, b = thirds(inverse), thirds(flat[...])
    pairs = ((0, 0), (0, 1), (1, 0), (1, 1), (0, 2), (2, 0))
    left = jnp.concatenate([a[i] for i, _ in pairs], axis=1)
    right = jnp.concatenate([b[j] for _, j in pairs], axis=0)
    solved = jnp.dot(left, right, preferred_element_type=f32)
    for r in range(16):
        basis[pl.ds(r, 64, stride=16)] = solved[:, r * 128:(r + 1) * 128]


def shape(*dims):
    return jax.ShapeDtypeStruct(dims, f32)


def call(kernel, outs, *args, scratch=(), sems=0, places=None, limit=32 * 1024 * 1024, flops=0, alias={}, name):
    spec = pl.BlockSpec(memory_space=pltpu.VMEM)
    many = isinstance(outs, tuple)
    return pl.pallas_call(
        kernel,
        out_shape=outs,
        in_specs=[pl.BlockSpec(memory_space=p) for p in places or [pltpu.VMEM] * len(args)],
        out_specs=tuple([spec] * len(outs)) if many else spec,
        scratch_shapes=[pltpu.VMEM(s, f32) for s in scratch] + [pltpu.SemaphoreType.DMA((sems,))] * (sems > 0),
        compiler_params=pltpu.CompilerParams(vmem_limit_bytes=limit),
        cost_estimate=pl.CostEstimate(flops=1024, bytes_accessed=1024, transcendentals=0),
        input_output_aliases=alias,
        name=name,
    )(*args)


def shards(probes, conduct, storage):
    probes, conduct, storage = probes.reshape(64, 16, 128), conduct.reshape(16, 128), storage.reshape(16, 128)
    sent = call(
        send_kernel,
        shape(32, CHUNK, 128),
        probes,
        conduct,
        storage,
        scratch=(probes.shape, conduct.shape, storage.shape),
        sems=3,
        places=[pltpu.HBM] * 3,
        limit=None,
        name="send",
    )
    got = lax.all_to_all(sent, ("ty", "tx", "tc"), 0, 0, tiled=True)
    field = shape(OWN, 8, 8, 128)
    got = got.reshape(32 * CHUNK, 128)
    half, first = call(pack_kernel, (shape(OWN, 4, 8, 128), field), got, name="pack")
    exchanges = [[(i, i + 1) for i in range(k, 7, 2)] for k in range(2)]
    exchanges = [e + [(j, i) for i, j in e] for e in exchanges]

    def sides(a):
        return [a] + [lax.ppermute(a, "tz", e) for e in exchanges]

    def swap(a):
        return lax.ppermute(a, "tc", [(0, 1), (1, 0)])

    halfs = sides(half)
    fields = [sides(first)]
    second = call(pack_second_kernel, field, got, fields[0][1], places=[pltpu.VMEM, pl.ANY], name="pack2")
    fields.append(sides(second))
    wide = shape(EXT, 8, 8, 128)
    coefs = call(coef_kernel, (wide, wide), *halfs, *[swap(a) for a in halfs], name="coef")
    pads = ((EXT, 10, 8, 128),) * 2
    work = 14 * 120 * 8 * 1024
    forward = [
        call(forward_kernel, field, *f, *coefs, scratch=(wide.shape,) + pads, flops=work, name="forward") for f in fields
    ]
    forward = [sides(f) for f in forward]
    scratch = (field.shape,) + pads
    summed = call(
        functools.partial(adjoint_kernel, 0), shape(1024, 128), *forward[0], *coefs, scratch=scratch, flops=work, name="adjoint1"
    )
    summed = call(
        functools.partial(adjoint_kernel, 1),
        shape(1024, 128),
        *forward[1],
        *coefs,
        summed,
        scratch=scratch,
        flops=work,
        alias={5: 0},
        name="adjoint2",
    )
    back = lax.all_to_all(summed.reshape(32, 32, 128), ("ty", "tx", "tc"), 0, 0, tiled=True)
    flat, gram = call(
        gram_kernel,
        (shape(64, 2048), shape(24, 128)),
        back.reshape(1024, 128),
        probes.reshape(1024, 128),
        storage,
        name="gram",
    )
    gram = gram + swap(gram)
    parts = lax.all_to_all(jnp.broadcast_to(gram[None], (16, 24, 128)), ("ty", "tx"), 0, 0, tiled=True)
    parts = lax.all_to_all(jnp.broadcast_to(parts.sum(0)[None], (8, 24, 128)), "tz", 0, 0, tiled=True)
    scale = math.sqrt(64 * 64 * 128)

    def solve(*refs):
        solve_kernel(*refs, scale)

    basis, factor = call(solve, (shape(1024, 128), shape(64, 64)), parts, flat, name="solve")
    return basis.reshape(64, 2, 8, 128), factor


def solution(mesh):
    fine = Mesh(mesh.devices.reshape(4, 4, 2, 8), ("ty", "tx", "tc", "tz"))
    gx = ("ty", "tx", "tc")
    placed = (P(None, gx, "tz", None), P(gx, "tz", None), P(gx, "tz", None))
    return jax.shard_map(
        shards,
        mesh=fine,
        in_specs=placed,
        out_specs=(P(None, gx, "tz", None), P()),
        check_vma=False,
    )
```
